32 devices in a mesh: fsdp: 32 (over z, y, x, core).
Axes of the slice: x: 2, y: 2, z: 4, core: 2. Of those that a mesh axis runs over, the one named last changes fastest.
Arguments:
- inputs: bfloat16 [16384, 1024], P('fsdp'), may hold values from -6 to 6
- seq_lens: int32 [32, 8], P('fsdp'), may hold values from 0 to 512, as said below
- mixer_gain: bfloat16 [1024], P('fsdp'), may hold values from 0.5 to 1.5
- input_proj: bfloat16 [1024, 3072], P('fsdp'), may hold values from -0.1875 to 0.1875
- conv_taps: bfloat16 [3072, 4], P('fsdp'), may hold values from -3 to 3
- rate_proj: bfloat16 [1024, 12], P('fsdp'), may hold values from -0.1875 to 0.1875
- decay_params: float32 [2, 6], replicated, may hold values from -6.5 to 1, as said below
- outgate_proj: bfloat16 [1024, 1536], P('fsdp'), may hold values from -0.1875 to 0.1875
- head_gain: float32 [256], replicated, may hold values from 0.5 to 1.5
- output_proj: bfloat16 [1536, 1024], P('fsdp'), may hold values from -0.15625 to 0.15625
- feed_gain: bfloat16 [1024], P('fsdp'), may hold values from 0.5 to 1.5
- gate_proj: bfloat16 [1024, 2816], P('fsdp'), may hold values from -0.1875 to 0.1875
- up_proj: bfloat16 [1024, 2816], P('fsdp'), may hold values from -0.1875 to 0.1875
- down_proj: bfloat16 [2816, 1024], P('fsdp'), may hold values from -0.109375 to 0.109375
- cotangent: bfloat16 [16384, 1024], P('fsdp'), may hold values from -6 to 6
Outputs:
- output: bfloat16 [16384, 1024], P('fsdp')
- grad_inputs: float32 [16384, 1024], P('fsdp')
- grad_mixer_gain: float32 [1024], P('fsdp')
- grad_input_proj: float32 [1024, 3072], P('fsdp')
- grad_conv_taps: float32 [3072, 4], P('fsdp')
- grad_rate_proj: float32 [1024, 12], P('fsdp')
- grad_decay_params: float32 [2, 6], replicated
- grad_outgate_proj: float32 [1024, 1536], P('fsdp')
- grad_head_gain: float32 [256], replicated
- grad_output_proj: float32 [1536, 1024], P('fsdp')
- grad_feed_gain: float32 [1024], P('fsdp')
- grad_gate_proj: float32 [1024, 2816], P('fsdp')
- grad_up_proj: float32 [1024, 2816], P('fsdp')
- grad_down_proj: float32 [2816, 1024], P('fsdp')
The draws below stay inside these ranges and needn't reach their ends.
Inputs may be any that keep to these rules, and one draw needn't show every extreme that they name: `seq_lens`: row d lists the lengths of the sequences on device d in the order in which they lie, nonzero entries first and zeros after them. Each device's lengths, each rounded up to a multiple of 64, add up to at most 512, and on some device to exactly 512; some sequence has exactly 512 tokens. `decay_params`: row 0 holds each head's logarithm of the decay scale, row 1 its decay bias.
All inputs are finite; a program needn't handle non-finite values.
Results may differ from the reference program's by a relative error of at most 0.02.
The reference program's roundings to bfloat16 on the way count: a program that leaves them out, or rounds other values in their place, can miss the bound.
Values may be sent and summed in bfloat16 or wider, within the bound.
A program may use at most 256 MiB of HBM per device.

```python
import jax
import jax.numpy as jnp
from jax import lax

D = 1024
NH = 6
DK = 128
DV = 256
FF = 2816
CONV = 4
GROUP = 64
SEQ_MAX = 512
TOK_DEV = 512
QKV = 3072
VD = 1536
TOKENS = 16384
N_FSDP = 32


def draw_seq_lens(key, part):
    key = jax.random.fold_in(key, 11)
    keys_all = jax.random.split(key, 4)
    blocks = TOK_DEV // GROUP
    longest = SEQ_MAX // GROUP
    budget = jax.random.randint(keys_all[0], (N_FSDP,), max(blocks // 4, 1), blocks + 1)
    fullest = jax.random.randint(keys_all[1], (), 0, N_FSDP)
    device_ids = jnp.arange(N_FSDP)
    budget = jnp.where(device_ids == fullest, blocks, budget)
    pieces = jax.random.randint(keys_all[2], (N_FSDP, blocks), 1, longest + 1)
    first_slot = (device_ids[:, None] == fullest) & (jnp.arange(blocks)[None, :] == 0)
    pieces = jnp.where(first_slot, longest, pieces)
    before = jnp.cumsum(pieces, axis=1) - pieces
    taken_blocks = jnp.clip(budget[:, None] - before, 0, pieces)
    short_by = jax.random.randint(keys_all[3], (N_FSDP, blocks), 0, GROUP)
    short_by = jnp.where(first_slot, 0, short_by)
    return jnp.where(taken_blocks > 0, taken_blocks * GROUP - short_by, 0).astype(jnp.int32)


def draw_decay_params(key, part):
    key = jax.random.fold_in(key, 23)
    scale_key, bias_key = jax.random.split(key)
    log_scale = jax.random.uniform(scale_key, (NH,), jnp.float32, -6.5, -2.5)
    offsets = jax.random.uniform(bias_key, (NH,), jnp.float32, -1.0, 1.0)
    return jnp.stack([log_scale, offsets])


def level_of(stream_key, shape, cuts, smallest, high):
    level = 1.0
    for dim, blocks in cuts:
        steps = jax.random.uniform(jax.random.fold_in(jax.random.fold_in(stream_key, 6), dim), (blocks,), jnp.float32, smallest / len(cuts), high / len(cuts))
        level = level * jnp.repeat(jnp.exp(steps), shape[dim] // blocks).reshape((-1,) + (1,) * (len(shape) - 1 - dim))
    return level


def gaussian(rng, extent, spread, most, cuts=(), kind=jnp.bfloat16):
    factor_of = level_of(rng, extent, cuts, -0.22, 0.18) if cuts else 1.0
    values = jax.random.normal(rng, extent, jnp.float32) * spread * factor_of
    return jnp.minimum(jnp.maximum(values, -most), most).astype(kind)


def setup_inputs(seed: int = 0) -> dict:
    key_of = jax.random.split(jax.random.key(seed), 16)
    inputs = gaussian(key_of[0], (TOKENS, D), 1.0, 6.0, ((0, 32),))
    seq_lens = draw_seq_lens(jax.random.fold_in(key_of[15], 71), 0)
    mixer_gain = jnp.clip(1.0 + 0.1 * jax.random.normal(key_of[2], (D,), jnp.float32), 0.5, 1.5).astype(jnp.bfloat16)
    input_proj = gaussian(key_of[3], (D, QKV), D ** -0.5, 0.1875, ((0, 32),))
    conv_taps = gaussian(key_of[4], (QKV, CONV), CONV ** -0.5, 3.0, ((0, 32),))
    rate_proj = gaussian(key_of[5], (D, 2 * NH), D ** -0.5, 0.1875, ((0, 32),))
    decay_params = draw_decay_params(jax.random.fold_in(key_of[15], 71), 0)
    outgate_proj = gaussian(key_of[7], (D, VD), D ** -0.5, 0.1875, ((0, 32),))
    head_gain = jnp.clip(1.0 + 0.1 * jax.random.normal(key_of[8], (DV,), jnp.float32), 0.5, 1.5)
    output_proj = gaussian(key_of[9], (VD, D), VD ** -0.5, 0.15625, ((0, 32),))
    feed_gain = jnp.clip(1.0 + 0.1 * jax.random.normal(key_of[10], (D,), jnp.float32), 0.5, 1.5).astype(jnp.bfloat16)
    gate_proj = gaussian(key_of[11], (D, FF), D ** -0.5, 0.1875, ((0, 32),))
    up_proj = gaussian(key_of[12], (D, FF), D ** -0.5, 0.1875, ((0, 32),))
    down_proj = gaussian(key_of[13], (FF, D), FF ** -0.5, 0.109375, ((0, 32),))
    cotangent = gaussian(key_of[14], (TOKENS, D), 1.0, 6.0, ((0, 32),))
    return {"inputs": inputs, "seq_lens": seq_lens, "mixer_gain": mixer_gain, "input_proj": input_proj, "conv_taps": conv_taps, "rate_proj": rate_proj, "decay_params": decay_params, "outgate_proj": outgate_proj, "head_gain": head_gain, "output_proj": output_proj, "feed_gain": feed_gain, "gate_proj": gate_proj, "up_proj": up_proj, "down_proj": down_proj, "cotangent": cotangent}


EPS = 1e-06
HIGH = lax.Precision.HIGHEST

@jax.custom_vjp
def low(v):
    return lax.optimization_barrier(v.astype(jnp.bfloat16)).astype(jnp.float32)

@jax.custom_vjp
def low_back(v):
    return v

def low_keep(v):
    return (low(v), None)

def low_pass(kept, grad):
    return (grad,)

def back_keep(v):
    return (v, None)

def back_low(kept, grad):
    return (low(grad),)
low.defvjp(low_keep, low_pass)
low_back.defvjp(back_keep, back_low)

def matmul(left, right):
    return jnp.dot(left.astype(jnp.float32), right.astype(jnp.float32), precision=HIGH, preferred_element_type=jnp.float32)

def rms_norm(values, norm_gain):
    return values * lax.rsqrt(lax.optimization_barrier(jnp.mean(values * values, axis=-1, keepdims=True)) + EPS) * norm_gain

def layout(lengths, row_count):
    padded = ((lengths + GROUP - 1) // GROUP * GROUP).astype(jnp.int32)
    starts = (jnp.cumsum(padded) - padded).astype(jnp.int32)
    offset = jnp.arange(row_count, dtype=jnp.int32)[:, None] - starts[None, :]
    inside = (offset >= 0) & (offset < padded[None, :])
    live_rows = lax.optimization_barrier(jnp.sum(jnp.where(inside & (offset < lengths[None, :]), 1.0, 0.0), axis=1)).astype(jnp.float32)
    position = lax.optimization_barrier(jnp.sum(jnp.where(inside, offset, 0), axis=1)).astype(jnp.int32)
    return (live_rows, position)

def short_conv(mixed_rows, tap_values, position):
    summed = mixed_rows * tap_values[:, CONV - 1]
    for distance in range(1, CONV):
        shifted = jnp.concatenate([jnp.zeros((distance, mixed_rows.shape[1]), mixed_rows.dtype), mixed_rows[:-distance]], axis=0)
        summed = summed + jnp.where((position >= distance)[:, None], shifted, 0.0) * tap_values[:, CONV - 1 - distance]
    return summed

def qkv_heads(mixed_rows, tap_values, position):
    row_count = mixed_rows.shape[0]
    activated = jax.nn.silu(short_conv(mixed_rows, tap_values, position))
    queries = activated[:, :NH * DK].reshape(row_count, NH, DK)
    keys = activated[:, NH * DK:2 * NH * DK].reshape(row_count, NH, DK)
    values = activated[:, 2 * NH * DK:].reshape(row_count, NH, DV)
    queries = queries * lax.rsqrt(lax.optimization_barrier(jnp.sum(queries * queries, axis=-1, keepdims=True)) + EPS) * DK ** (-0.5)
    keys = keys * lax.rsqrt(lax.optimization_barrier(jnp.sum(keys * keys, axis=-1, keepdims=True)) + EPS)
    return (queries, keys, values)

def gates(rate_logits, decay_params, live_rows):
    write_rate = jax.nn.sigmoid(rate_logits[:, :NH]) * live_rows[:, None]
    log_decay = -jnp.exp(decay_params[0]) * jax.nn.softplus(rate_logits[:, NH:] + decay_params[1]) * live_rows[:, None]
    return (write_rate, log_decay)

def group_step(state, block):
    queries, keys, values, write_rate, log_decay, restart = block
    state = state * (1.0 - restart)
    block_len = queries.shape[0]
    total_decay = jnp.cumsum(log_decay, axis=0)
    lower = jnp.tril(jnp.ones((block_len, block_len), jnp.float32))
    identity = jnp.eye(block_len, dtype=jnp.float32)
    strict = lower - identity
    gaps = total_decay.T[:, :, None] - total_decay.T[:, None, :]
    within = jnp.exp(jnp.where(lower > 0, gaps, 0.0)) * lower
    key_key = jnp.einsum('thd,ihd->hti', keys, keys, precision=HIGH)
    coupling = write_rate.T[:, :, None] * within * key_key * strict
    start_key = jnp.einsum('thd,hde->hte', keys, state, precision=HIGH)
    scaled = (write_rate * jnp.exp(total_decay)).T[:, :, None]
    target = write_rate.T[:, :, None] * values.transpose(1, 0, 2) - scaled * start_key
    pseudo = jax.scipy.linalg.solve_triangular(identity + coupling, target, lower=True)
    query_key = jnp.einsum('thd,ihd->hti', queries, keys, precision=HIGH) * within
    start_query = jnp.einsum('thd,hde->hte', queries, state, precision=HIGH)
    outputs = jnp.exp(total_decay).T[:, :, None] * start_query + jnp.einsum('hti,hie->hte', query_key, pseudo, precision=HIGH)
    tail_decay = jnp.exp(total_decay[-1][None, :] - total_decay)
    state = jnp.exp(total_decay[-1])[:, None, None] * state + jnp.einsum('ihd,ih,hie->hde', keys, tail_decay, pseudo, precision=HIGH)
    return (state, outputs.transpose(1, 0, 2))

def delta_rule(queries, keys, values, write_rate, log_decay, position):
    row_count = queries.shape[0]
    blocks = row_count // GROUP

    def to_blocks(array):
        return array.reshape((blocks, GROUP) + array.shape[1:])
    restart = jnp.where(position.reshape(blocks, GROUP)[:, 0] == 0, 1.0, 0.0).astype(jnp.float32)
    initial = jnp.zeros((NH, DK, DV), jnp.float32)
    last_state, outputs = lax.scan(jax.checkpoint(group_step), initial, (to_blocks(queries), to_blocks(keys), to_blocks(values), to_blocks(write_rate), to_blocks(log_decay), restart))
    return outputs.reshape(row_count, NH, DV)

def mixer_core(queries, keys, values, rate_logits, decay_params, live_rows, position):
    write_rate, log_decay = gates(rate_logits, decay_params, live_rows)
    return delta_rule(queries, keys, values, write_rate, log_decay, position)

def gated_norm(recurrent, gate_logits, head_gain):
    row_count = recurrent.shape[0]
    return rms_norm(recurrent, head_gain) * jax.nn.silu(gate_logits.reshape(row_count, NH, DV))

def buffer_forward(params, stream, lengths):
    mixer_gain, input_proj, conv_taps, rate_proj, decay_params, outgate_proj, head_gain, output_proj, feed_gain, gate_proj, up_proj, down_proj = params
    row_count = stream.shape[0]
    live_rows, position = layout(lengths, row_count)
    normed = low(rms_norm(stream, mixer_gain))
    mixed_in = low_back(matmul(normed, input_proj))
    rate_logits = low_back(matmul(normed, rate_proj))
    gate_logits = low_back(matmul(normed, outgate_proj))
    queries, keys, values = qkv_heads(mixed_in, conv_taps, position)
    recurrent = mixer_core(low(queries), low(keys), low(values), rate_logits, decay_params, live_rows, position)
    head_out = low(gated_norm(recurrent, gate_logits, head_gain).reshape(row_count, NH * DV))
    middle = stream + low_back(matmul(head_out, output_proj))
    normed_two = low(rms_norm(middle, feed_gain))
    gate_act = low_back(matmul(normed_two, gate_proj))
    up_act = low_back(matmul(normed_two, up_proj))
    hidden = low(jax.nn.silu(gate_act) * up_act)
    return (middle + low_back(matmul(hidden, down_proj))) * live_rows[:, None]

def reference(inputs, seq_lens, mixer_gain, input_proj, conv_taps, rate_proj, decay_params, outgate_proj, head_gain, output_proj, feed_gain, gate_proj, up_proj, down_proj, cotangent):
    params = tuple((argument.astype(jnp.float32) for argument in (mixer_gain, input_proj, conv_taps, rate_proj, decay_params, outgate_proj, head_gain, output_proj, feed_gain, gate_proj, up_proj, down_proj)))
    block_fn = jax.checkpoint(buffer_forward)

    def forward(stream, weights):
        buffers = stream.reshape(N_FSDP, TOK_DEV, D)

        def visit(running, element):
            return (running, block_fn(weights, element[0], element[1]))
        running_out, results = lax.scan(visit, jnp.zeros((), jnp.float32), (buffers, seq_lens))
        return results.reshape(N_FSDP * TOK_DEV, D)
    result, pullback = jax.vjp(forward, inputs.astype(jnp.float32), params)
    grad_stream, grads = pullback(cotangent.astype(jnp.float32))
    return (result.astype(jnp.bfloat16), grad_stream, grads[0], grads[1], grads[2], grads[3], grads[4], grads[5], grads[6], grads[7], grads[8], grads[9], grads[10], grads[11])
```

```python
import jax
import jax.numpy as jnp
from jax import lax
from jax.experimental import pallas as pl
from jax.experimental.pallas import tpu as pltpu
from jax.sharding import PartitionSpec as P

NH = 6
DK = 128
DV = 256
CONV = 4
GROUP = 64
PIECE = 512


EPS = 1e-06


def rms_norm(values, norm_gain):
    return values * lax.rsqrt(jnp.mean(values * values, axis=-1, keepdims=True) + EPS) * norm_gain


def layout(lengths, row_count):
    padded = (lengths + GROUP - 1) // GROUP * GROUP
    starts = jnp.cumsum(padded) - padded
    offset = jnp.arange(row_count, dtype=jnp.int32)[:, None] - starts[None, :]
    inside = (offset >= 0) & (offset < padded[None, :])
    live_rows = jnp.sum(jnp.where(inside & (offset < lengths[None, :]), 1.0, 0.0), axis=1).astype(
        jnp.float32
    )
    position = jnp.sum(jnp.where(inside, offset, 0), axis=1)
    return (live_rows, position)


def short_conv(mixed_rows, tap_values, position):
    summed = mixed_rows * tap_values[:, CONV - 1]
    for distance in range(1, CONV):
        shifted = jnp.concatenate(
            [jnp.zeros((distance, mixed_rows.shape[1]), mixed_rows.dtype), mixed_rows[:-distance]],
            axis=0,
        )
        summed = (
            summed
            + jnp.where((position >= distance)[:, None], shifted, 0.0)
            * tap_values[:, CONV - 1 - distance]
        )
    return summed


def qkv_heads(mixed_rows, tap_values, position):
    row_count = mixed_rows.shape[0]
    activated = jax.nn.silu(short_conv(mixed_rows, tap_values, position))
    queries = activated[:, : NH * DK].reshape(row_count, NH, DK)
    keys = activated[:, NH * DK : 2 * NH * DK].reshape(row_count, NH, DK)
    values = activated[:, 2 * NH * DK :].reshape(row_count, NH, DV)
    queries = (
        queries * lax.rsqrt(jnp.sum(queries * queries, axis=-1, keepdims=True) + EPS) * DK ** (-0.5)
    )
    keys = keys * lax.rsqrt(jnp.sum(keys * keys, axis=-1, keepdims=True) + EPS)
    return (queries, keys, values)


def gates(rate_logits, decay_params, live_rows):
    write_rate = jax.nn.sigmoid(rate_logits[:, :NH]) * live_rows[:, None]
    log_decay = (
        -jnp.exp(decay_params[0])
        * jax.nn.softplus(rate_logits[:, NH:] + decay_params[1])
        * live_rows[:, None]
    )
    return (write_rate, log_decay)


ROWS_COLS = (((1,), (0,)), ((), ()))
COLS_COLS = (((1,), (1,)), ((), ()))
ROWS_ROWS = (((0,), (0,)), ((), ()))


def product(left, right, dims=ROWS_COLS):
    return lax.dot_general(
        left.astype(jnp.bfloat16),
        right.astype(jnp.bfloat16),
        dims,
        preferred_element_type=jnp.float32,
    )


def halves(values):
    high = values.astype(jnp.bfloat16)
    return (high, (values - high.astype(jnp.float32)).astype(jnp.bfloat16))


def right_split(left, right, dims=ROWS_COLS):
    high, rest = halves(right)
    return product(left, high, dims) + product(left, rest, dims)


def left_split(left, right, dims=ROWS_COLS):
    high, rest = halves(left)
    return product(high, right, dims) + product(rest, right, dims)


def triple(left, right, dims=ROWS_COLS):
    left_high, left_rest = halves(left)
    right_high, right_rest = halves(right)
    return (
        product(left_high, right_high, dims)
        + product(left_high, right_rest, dims)
        + product(left_rest, right_high, dims)
    )


def head_slice(ref, head, width):
    return ref[:, head * width : (head + 1) * width]


def triangle():
    row = lax.broadcasted_iota(jnp.int32, (GROUP, GROUP), 0)
    column = lax.broadcasted_iota(jnp.int32, (GROUP, GROUP), 1)
    return (row, column)


def core_forward_kernel(
    restart_ref, q_ref, k_ref, v_ref, scal_ref, decay_ref, out_ref, start_ref, inv_ref, pseudo_ref, state
):
    step = pl.program_id(0)

    @pl.when(step == 0)
    def _():
        state[...] = jnp.zeros_like(state)

    keep = 1.0 - restart_ref[step]
    row, column = triangle()
    lower = row >= column
    strict = row > column
    identity = jnp.where(row == column, 1.0, 0.0)
    withins = []
    couplings = []
    query_keys = []
    inverses = []
    heads = range(NH)
    for head in heads:
        queries = head_slice(q_ref, head, DK)
        keys = head_slice(k_ref, head, DK)
        write = scal_ref[:, head : head + 1]
        decay = scal_ref[:, NH + head : NH + head + 1]
        gaps = decay - decay_ref[0, head : head + 1, :]
        within = jnp.where(lower, jnp.exp(jnp.where(lower, gaps, 0.0)), 0.0)
        both = product(jnp.concatenate([keys, queries], axis=0), keys, COLS_COLS)
        coupling = jnp.where(strict, write * within * both[:GROUP], 0.0)
        couplings.append(coupling)
        query_keys.append(both[GROUP:] * within)
        pair = (row == column + 1) & (row % 2 == 1)
        inverses.append(identity - jnp.where(pair, coupling, 0.0))
    size = 2
    while size < GROUP:
        below = (row // size) % 2 == 1
        pair = below & (row // size == column // size + 1)
        firsts = [triple(inverses[head], jnp.where(pair, couplings[head], 0.0)) for head in heads]
        inverses = [inverses[head] - triple(firsts[head], inverses[head]) for head in heads]
        size = size * 2
    for head in heads:
        queries = head_slice(q_ref, head, DK)
        keys = head_slice(k_ref, head, DK)
        values = head_slice(v_ref, head, DV).astype(jnp.float32)
        write = scal_ref[:, head : head + 1]
        decay = scal_ref[:, NH + head : NH + head + 1]
        grown = jnp.exp(decay)
        start = state[head] * keep
        start_ref[0, head] = start
        inv_ref[0, head] = inverses[head]
        both = right_split(jnp.concatenate([keys, queries], axis=0), start)
        target = write * values - write * grown * both[:GROUP]
        pseudo = triple(inverses[head], target)
        pseudo_ref[:, head * DV : (head + 1) * DV] = pseudo
        out_ref[:, head * DV : (head + 1) * DV] = grown * both[GROUP:] + triple(
            query_keys[head], pseudo
        )
        last = decay[GROUP - 1 :, :]
        tail = jnp.exp(last - decay)
        state[head] = jnp.exp(last) * start + right_split(keys, tail * pseudo, ROWS_ROWS)


def core_backward_kernel(
    restart_ref,
    q_ref,
    k_ref,
    v_ref,
    scal_ref,
    decay_ref,
    start_ref,
    inv_ref,
    pseudo_ref,
    dout_ref,
    dq_ref,
    dk_ref,
    dv_ref,
    dscal_ref,
    ddecay_ref,
    costate,
):
    step = pl.program_id(0)

    @pl.when(step == 0)
    def _():
        costate[...] = jnp.zeros_like(costate)

    keep = 1.0 - restart_ref[pl.num_programs(0) - 1 - step]
    row, column = triangle()
    lower = row >= column
    strict = row > column
    final = lax.broadcasted_iota(jnp.int32, (GROUP, 1), 0) == GROUP - 1
    ddecay_ref[...] = jnp.zeros_like(ddecay_ref)
    for head in range(NH):
        queries = head_slice(q_ref, head, DK)
        keys = head_slice(k_ref, head, DK)
        values = head_slice(v_ref, head, DV).astype(jnp.float32)
        wide_keys = keys.astype(jnp.float32)
        wide_queries = queries.astype(jnp.float32)
        write = scal_ref[:, head : head + 1]
        decay = scal_ref[:, NH + head : NH + head + 1]
        start = start_ref[0, head]
        pseudo = head_slice(pseudo_ref, head, DV)
        dout = head_slice(dout_ref, head, DV)
        dstate = costate[head]
        gaps = decay - decay_ref[0, head : head + 1, :]
        within = jnp.where(lower, jnp.exp(jnp.where(lower, gaps, 0.0)), 0.0)
        keys_queries = jnp.concatenate([keys, queries], axis=0)
        both = product(keys_queries, keys, COLS_COLS)
        key_key = jnp.where(strict, both[:GROUP] * within, 0.0)
        query_key = both[GROUP:] * within
        grown = jnp.exp(decay)
        last = decay[GROUP - 1 :, :]
        tail = jnp.exp(last - decay)
        dpseudo = triple(query_key, dout, ROWS_ROWS) + tail * right_split(keys, dstate)
        dtarget = triple(inv_ref[0, head], dpseudo, ROWS_ROWS)
        stacked = jnp.concatenate([dtarget, dout], axis=0)
        pairs = triple(stacked, pseudo, COLS_COLS)
        dcoupling = jnp.where(strict, -pairs[:GROUP], 0.0)
        dquery_key = jnp.where(lower, pairs[GROUP:], 0.0)
        reads = triple(stacked, start, COLS_COLS)
        dread_key = reads[:GROUP]
        dq_state = grown * reads[GROUP:]
        inner = dquery_key * within
        dkey_key = dcoupling * write * within
        dq_ref[:, head * DK : (head + 1) * DK] = dq_state + left_split(inner, keys)
        scaled = write * grown
        dtail = tail * triple(pseudo, dstate, COLS_COLS)
        dk_ref[:, head * DK : (head + 1) * DK] = (
            left_split(jnp.concatenate([dkey_key, inner], axis=0), keys_queries, ROWS_ROWS)
            + left_split(dkey_key, keys)
            - scaled * dread_key
            + dtail
        )
        dv_ref[:, head * DV : (head + 1) * DV] = write * dtarget
        read_key = jnp.sum(dread_key * wide_keys, axis=1, keepdims=True)
        dscal_ref[:, head : head + 1] = (
            jnp.sum(dtarget * values, axis=1, keepdims=True)
            - grown * read_key
            + jnp.sum(dcoupling * key_key, axis=1, keepdims=True)
        )
        weight = dquery_key * query_key + dcoupling * write * key_key
        moved = jnp.sum(dtail * wide_keys, axis=1, keepdims=True)
        at_last = jnp.sum(moved, axis=0, keepdims=True) + jnp.exp(last) * jnp.sum(
            jnp.sum(start * dstate, axis=1, keepdims=True), axis=0, keepdims=True
        )
        dscal_ref[:, NH + head : NH + head + 1] = (
            jnp.sum(dq_state * wide_queries, axis=1, keepdims=True)
            - scaled * read_key
            + jnp.sum(weight, axis=1, keepdims=True)
            - moved
            + jnp.where(final, at_last, 0.0)
        )
        ddecay_ref[0, head : head + 1, :] = -jnp.sum(weight, axis=0, keepdims=True)
        sources = jnp.concatenate([-scaled * dtarget, grown * dout], axis=0)
        costate[head] = keep * (
            jnp.exp(last) * dstate + right_split(keys_queries, sources, ROWS_ROWS)
        )


def core_specs(blocks, backward):
    def at(step):
        return blocks - 1 - step if backward else step

    def rows(width):
        return pl.BlockSpec((GROUP, width), lambda step: (at(step), 0))

    def lead(*shape):
        return pl.BlockSpec((1,) + shape, lambda step: (at(step),) + (0,) * len(shape))

    return rows, lead


def core_forward(restart, queries, keys, values, scalars, decay_rows):
    row_count = queries.shape[0]
    blocks = row_count // GROUP
    rows, lead = core_specs(blocks, False)
    wide = jax.ShapeDtypeStruct((row_count, NH * DV), jnp.float32)
    return pl.pallas_call(
        core_forward_kernel,
        grid=(blocks,),
        in_specs=[
            pl.BlockSpec(memory_space=pltpu.SMEM),
            rows(NH * DK),
            rows(NH * DK),
            rows(NH * DV),
            rows(2 * NH),
            lead(8, GROUP),
        ],
        out_specs=[rows(NH * DV), lead(NH, DK, DV), lead(NH, GROUP, GROUP), rows(NH * DV)],
        out_shape=[
            wide,
            jax.ShapeDtypeStruct((blocks, NH, DK, DV), jnp.float32),
            jax.ShapeDtypeStruct((blocks, NH, GROUP, GROUP), jnp.float32),
            wide,
        ],
        scratch_shapes=[pltpu.VMEM((NH, DK, DV), jnp.float32)],
        compiler_params=pltpu.CompilerParams(vmem_limit_bytes=24 * 2**20),
        cost_estimate=pl.CostEstimate(
            flops=40_000_000_000, bytes_accessed=20_000_000, transcendentals=400_000
        ),
    )(restart, queries, keys, values, scalars, decay_rows)


def core_backward(restart, queries, keys, values, scalars, decay_rows, kept, d_recurrent):
    row_count = queries.shape[0]
    blocks = row_count // GROUP
    rows, lead = core_specs(blocks, True)
    narrow = jax.ShapeDtypeStruct((row_count, NH * DK), jnp.float32)
    return pl.pallas_call(
        core_backward_kernel,
        grid=(blocks,),
        in_specs=[
            pl.BlockSpec(memory_space=pltpu.SMEM),
            rows(NH * DK),
            rows(NH * DK),
            rows(NH * DV),
            rows(2 * NH),
            lead(8, GROUP),
            lead(NH, DK, DV),
            lead(NH, GROUP, GROUP),
            rows(NH * DV),
            rows(NH * DV),
        ],
        out_specs=[
            rows(NH * DK),
            rows(NH * DK),
            rows(NH * DV),
            rows(2 * NH),
            lead(8, GROUP),
        ],
        out_shape=[
            narrow,
            narrow,
            jax.ShapeDtypeStruct((row_count, NH * DV), jnp.float32),
            jax.ShapeDtypeStruct((row_count, 2 * NH), jnp.float32),
            jax.ShapeDtypeStruct((blocks, 8, GROUP), jnp.float32),
        ],
        scratch_shapes=[pltpu.VMEM((NH, DK, DV), jnp.float32)],
        compiler_params=pltpu.CompilerParams(vmem_limit_bytes=24 * 2**20),
        cost_estimate=pl.CostEstimate(
            flops=40_000_000_000, bytes_accessed=20_000_000, transcendentals=400_000
        ),
    )(restart, queries, keys, values, scalars, decay_rows, *kept, d_recurrent)


def core_scalars(rate_logits, decay_params, live_rows):
    write_rate, log_decay = gates(rate_logits, decay_params, live_rows)
    blocks = log_decay.shape[0] // GROUP
    lower = jnp.tril(jnp.ones((GROUP, GROUP), jnp.float32))
    total = jnp.einsum(
        "ti,cih->cth",
        lower,
        log_decay.reshape(blocks, GROUP, NH),
        precision=lax.Precision.HIGHEST,
    )
    decay_rows = jnp.pad(total.transpose(0, 2, 1), ((0, 0), (0, 8 - NH), (0, 0)))
    return (jnp.concatenate([write_rate, total.reshape(-1, NH)], axis=1), decay_rows)


def gated_norm(recurrent, gate_logits, head_gain):
    row_count = recurrent.shape[0]
    return rms_norm(recurrent, head_gain) * jax.nn.silu(gate_logits.reshape(row_count, NH, DV))


def swiglu(gate_in, up_in):
    return jax.nn.silu(gate_in) * up_in


def by_owner(members, owners):
    return jnp.concatenate(
        [
            member[:, first : first + PIECE].reshape(owners, -1, PIECE)
            for member in members
            for first in range(0, member.shape[1], PIECE)
        ],
        axis=1,
    ).reshape(-1, PIECE)


def from_owner(joined, shapes):
    members = []
    first = 0
    for height, width in shapes:
        columns = []
        for _ in range(width // PIECE):
            columns.append(joined[first : first + height])
            first = first + height
        members.append(jnp.concatenate(columns, axis=1))
    return members


def shards(
    inputs,
    seq_lens,
    mixer_gain,
    input_proj,
    conv_taps,
    rate_proj,
    decay_params,
    outgate_proj,
    head_gain,
    output_proj,
    feed_gain,
    gate_proj,
    up_proj,
    down_proj,
    cotangent,
):
    row_count, width = inputs.shape
    owners = lax.axis_size("fsdp")
    live_rows, position = layout(seq_lens[0], row_count)
    restart = jnp.where(position.reshape(-1, GROUP)[:, 0] == 0, 1.0, 0.0).astype(jnp.float32)
    my_rows = mixer_gain.shape[0]
    qkv, gate_width, ff = input_proj.shape[1], outgate_proj.shape[1], gate_proj.shape[1]
    tap_flat = conv_taps.size // my_rows
    first_rate = qkv + gate_width
    first_tap = first_rate + 2 * NH
    used = first_tap + tap_flat + 2
    spare = -used % 128
    mixer_packed = jnp.concatenate(
        [
            input_proj,
            outgate_proj,
            rate_proj,
            conv_taps.reshape(my_rows, tap_flat),
            mixer_gain[:, None],
            feed_gain[:, None],
            jnp.zeros((my_rows, spare), jnp.bfloat16),
        ],
        axis=1,
    )
    full_mixer = lax.all_gather(mixer_packed, "fsdp", axis=0, tiled=True)
    feed_packed = jnp.concatenate([gate_proj, up_proj], axis=1)
    tall_packed = jnp.concatenate([output_proj, down_proj], axis=0)
    feed_packed, tall_packed, full_mixer = lax.optimization_barrier(
        (feed_packed, tall_packed, full_mixer)
    )
    full_tall = lax.all_gather(tall_packed, "fsdp", axis=0, tiled=False)
    full_feed = lax.all_gather(feed_packed, "fsdp", axis=0, tiled=True)
    out_rows = output_proj.shape[0]
    full_out = full_tall[:, :out_rows].reshape(-1, width)
    full_down = full_tall[:, out_rows:].reshape(-1, width)
    full_taps = full_mixer[:, first_tap : first_tap + tap_flat].reshape(-1, CONV)
    full_mgain = full_mixer[:, used - 2]
    full_fgain = full_mixer[:, used - 1]
    stream = inputs.astype(jnp.float32)
    normed_wide, norm_one_back = jax.vjp(rms_norm, stream, full_mgain.astype(jnp.float32))
    normed = normed_wide.astype(jnp.bfloat16)
    projected = jnp.dot(normed, full_mixer, preferred_element_type=jnp.float32)
    mixed_in = projected[:, :qkv]
    gate_logits = projected[:, qkv:first_rate]
    rate_logits = projected[:, first_rate:first_tap]

    def heads_fn(mixed_rows, tap_values):
        return qkv_heads(mixed_rows, tap_values, position)

    (queries, keys, values), heads_back = jax.vjp(heads_fn, mixed_in, full_taps.astype(jnp.float32))
    core_inputs = (
        restart,
        queries.reshape(row_count, NH * DK).astype(jnp.bfloat16),
        keys.reshape(row_count, NH * DK).astype(jnp.bfloat16),
        values.reshape(row_count, NH * DV).astype(jnp.bfloat16),
    )

    def scalars_fn(rate_in, param_in):
        return core_scalars(rate_in, param_in, live_rows)

    scalar_values, scalars_back = jax.vjp(scalars_fn, rate_logits, decay_params)
    recurrent_flat, *kept = core_forward(*core_inputs, *scalar_values)
    recurrent = recurrent_flat.reshape(row_count, NH, DV)
    head_normed, head_back = jax.vjp(gated_norm, recurrent, gate_logits, head_gain)
    head_out = head_normed.reshape(row_count, NH * DV).astype(jnp.bfloat16)
    middle = stream + jnp.dot(head_out, full_out, preferred_element_type=jnp.float32)
    normed_two_wide, norm_two_back = jax.vjp(rms_norm, middle, full_fgain.astype(jnp.float32))
    normed_two = normed_two_wide.astype(jnp.bfloat16)
    feed_act = jnp.dot(normed_two, full_feed, preferred_element_type=jnp.float32)
    gate_act = feed_act[:, :ff]
    up_act = feed_act[:, ff:]
    hidden_wide, swiglu_back = jax.vjp(swiglu, gate_act, up_act)
    hidden = hidden_wide.astype(jnp.bfloat16)
    output = (
        (middle + jnp.dot(hidden, full_down, preferred_element_type=jnp.float32))
        * live_rows[:, None]
    ).astype(jnp.bfloat16)
    d_final = cotangent.astype(jnp.float32) * live_rows[:, None]
    d_ffn = d_final.astype(jnp.bfloat16)
    d_hidden = jnp.einsum("rd,fd->rf", d_ffn, full_down, preferred_element_type=jnp.float32)
    d_gate_wide, d_up_wide = swiglu_back(d_hidden)
    d_feed = jnp.concatenate(
        [d_gate_wide.astype(jnp.bfloat16), d_up_wide.astype(jnp.bfloat16)], axis=1
    )
    grad_feed = jnp.einsum(
        "rd,rf->df", normed_two, d_feed, preferred_element_type=jnp.float32
    ).astype(jnp.bfloat16)
    d_normed_two = jnp.einsum("rf,df->rd", d_feed, full_feed, preferred_element_type=jnp.float32)
    d_middle_part, grad_fgain = norm_two_back(d_normed_two)
    d_middle = d_final + d_middle_part
    d_branch = d_middle.astype(jnp.bfloat16)
    grad_down = jnp.einsum("rf,rd->fd", hidden, d_ffn, preferred_element_type=jnp.float32)
    grad_out = jnp.einsum("rv,rd->vd", head_out, d_branch, preferred_element_type=jnp.float32)
    feed_joined = by_owner(
        (grad_feed, grad_out.astype(jnp.bfloat16), grad_down.astype(jnp.bfloat16)), owners
    )
    feed_joined, d_branch = lax.optimization_barrier((feed_joined, d_branch))
    feed_mine = lax.psum_scatter(feed_joined, "fsdp", scatter_dimension=0, tiled=True)
    d_head = jnp.einsum(
        "rd,vd->rv", d_branch, full_out, preferred_element_type=jnp.float32
    ).reshape(row_count, NH, DV)
    d_recurrent, d_gate_logits, grad_hgain = head_back(d_head)
    d_queries, d_keys, d_values, d_scalars, d_decay_rows = core_backward(
        *core_inputs, *scalar_values, kept, d_recurrent.reshape(row_count, NH * DV)
    )
    d_rates, grad_dparams = scalars_back((d_scalars, d_decay_rows))
    d_mixed, grad_taps = heads_back(
        (
            d_queries.reshape(row_count, NH, DK),
            d_keys.reshape(row_count, NH, DK),
            d_values.reshape(row_count, NH, DV),
        )
    )
    d_projected = jnp.concatenate(
        [
            d_mixed.astype(jnp.bfloat16),
            d_gate_logits.astype(jnp.bfloat16),
            d_rates.astype(jnp.bfloat16),
            jnp.zeros((row_count, tap_flat + 2 + spare), jnp.bfloat16),
        ],
        axis=1,
    )
    grad_mixer = jnp.einsum(
        "rd,rc->dc", normed, d_projected, preferred_element_type=jnp.float32
    ).astype(jnp.bfloat16)
    d_normed = jnp.einsum(
        "rc,dc->rd", d_projected, full_mixer, preferred_element_type=jnp.float32
    )
    d_stream, grad_mgain = norm_one_back(d_normed)
    grad_inputs = d_middle + d_stream
    mixer_mine = lax.psum_scatter(
        grad_mixer, "fsdp", scatter_dimension=0, tiled=True
    ).astype(jnp.float32)
    small = jnp.concatenate(
        [grad_taps.T.reshape(-1), grad_mgain, grad_fgain, grad_hgain, grad_dparams.reshape(-1)]
    )
    small_sum = lax.psum(small, "fsdp")
    me = lax.axis_index("fsdp")
    tap_rows = conv_taps.shape[0]
    taps_sum = small_sum[: qkv * CONV].reshape(CONV, qkv)
    gains_sum = small_sum[qkv * CONV : qkv * CONV + 2 * width].reshape(2, width)
    rest_sum = small_sum[qkv * CONV + 2 * width :]
    taps_mine = lax.dynamic_slice_in_dim(taps_sum, me * tap_rows, tap_rows, 1).T
    gains_mine = lax.dynamic_slice_in_dim(gains_sum, me * my_rows, my_rows, 1)
    gate_up_mine, out_mine, down_mine = from_owner(
        feed_mine.astype(jnp.float32),
        ((my_rows, 2 * ff), (out_rows, width), (down_proj.shape[0], width)),
    )
    return (
        output,
        grad_inputs,
        gains_mine[0],
        mixer_mine[:, :qkv],
        taps_mine,
        mixer_mine[:, first_rate:first_tap],
        rest_sum[head_gain.shape[0] :].reshape(2, NH),
        mixer_mine[:, qkv:first_rate],
        rest_sum[: head_gain.shape[0]],
        out_mine,
        gains_mine[1],
        gate_up_mine[:, :ff],
        gate_up_mine[:, ff:],
        down_mine,
    )


def solution(mesh):
    placed = (
        P("fsdp", None),
        P("fsdp", None),
        P("fsdp"),
        P("fsdp", None),
        P("fsdp", None),
        P("fsdp", None),
        P(),
        P("fsdp", None),
        P(),
        P("fsdp", None),
        P("fsdp"),
        P("fsdp", None),
        P("fsdp", None),
        P("fsdp", None),
        P("fsdp", None),
    )
    return jax.shard_map(
        shards,
        mesh=mesh,
        in_specs=placed,
        out_specs=(
            P("fsdp", None),
            P("fsdp", None),
            P("fsdp"),
            P("fsdp", None),
            P("fsdp", None),
            P("fsdp", None),
            P(),
            P("fsdp", None),
            P(),
            P("fsdp", None),
            P("fsdp"),
            P("fsdp", None),
            P("fsdp", None),
            P("fsdp", None),
        ),
        check_vma=False,
    )
```
